32 devices in a mesh: dp: 32 (over z, y, x, core).
Axes of the slice: x: 2, y: 2, z: 4, core: 2. Of those that a mesh axis runs over, the one named last changes fastest.
Arguments:
- tokens: bfloat16 [2, 24576, 768], P(None, 'dp'), may hold values from -6 to 6
- lengths: int32 [2, 128], P(None, 'dp'), may hold values from 16 to 720, as said below
- pairing: int32 [2, 64], replicated, may hold values from 0 to 63, each once within a row
- w_qkv: bfloat16 [768, 2304], replicated, may hold values from -0.21875 to 0.21875
- w_out: bfloat16 [768, 768], replicated, may hold values from -0.875 to 0.875
- w_gate_up: bfloat16 [768, 6144], replicated, may hold values from -0.21875 to 0.21875
- w_down: bfloat16 [3072, 768], replicated, may hold values from -0.109375 to 0.109375
- norm1_gain: float32 [768], replicated, may hold values from 0.5 to 1.5
- norm1_bias: float32 [768], replicated, may hold values from -0.6 to 0.6
- norm2_gain: float32 [768], replicated, may hold values from 0.5 to 1.5
- norm2_bias: float32 [768], replicated, may hold values from -0.6 to 0.6
Outputs:
- loss: float32 [2], replicated
- activations: bfloat16 [2, 24576, 768], P(None, 'dp')
- input_grad: float32 [2, 24576, 768], P(None, 'dp')
- grad_qkv: float32 [768, 2304], P('dp')
- grad_out: float32 [768, 768], P('dp')
- grad_gate_up: float32 [768, 6144], P('dp')
- grad_down: float32 [3072, 768], P('dp')
- grad_norm1_gain: float32 [768], P('dp')
- grad_norm1_bias: float32 [768], P('dp')
- grad_norm2_gain: float32 [768], P('dp')
- grad_norm2_bias: float32 [768], P('dp')
The draws below stay inside these ranges and needn't reach their ends.
Inputs may be any that keep to these rules, and one draw needn't show every extreme that they name: For each micro-batch and device, its 4 lengths sum to at most 768 and exactly 768 on at least a quarter of the devices; lengths are heavy-tailed and differ from device to device. Each micro-batch's row names every document once: query i's positive document is pairing[b, i].
All inputs are finite; a program needn't handle non-finite values.
Results may differ from the reference program's by a relative error of at most 0.0083.
Values sent between devices are 32-bit elements; how exact they have to be, the bound alone decides.
A program may use at most 320 MiB of HBM per device.

```python
import math
import jax
import jax.numpy as jnp
from jax import lax

D = 768
HEADS = 12
HEAD_DIM = 64
FF = 3072
TOK_DEV = 768
SEQ_DEV = 4
MIN_LEN = 16
MICRO = 2
TOKENS = 24576
NSEQ = 128
QUESTION_COUNT = 64
N_DP = 32


def draw_lengths(key, part):
    row_count = MICRO * NSEQ // SEQ_DEV
    key_exp, mask_scaler, key_fill, key_off = jax.random.split(key, 4)
    exponent = jax.random.randint(key_exp, (row_count, SEQ_DEV), 0, 7)
    multiplier = jax.random.randint(mask_scaler, (row_count, SEQ_DEV), 1, 4)
    weight = jnp.left_shift(multiplier, exponent)
    filled = jax.random.randint(key_fill, (row_count,), TOK_DEV // 2, TOK_DEV + 1)
    offset = jax.random.randint(key_off, (), 0, 4)
    row_ids = jnp.arange(row_count)
    filled = jnp.where((row_ids + offset) % 4 == 0, TOK_DEV, filled)
    longest_row = (4 - offset) % 4
    drop = (row_ids == longest_row)[:, None] & (jnp.arange(SEQ_DEV) > 0)[None, :]
    weight = jnp.where(drop, 0, weight)
    spare_tok = filled - SEQ_DEV * MIN_LEN
    share_tok = spare_tok[:, None] * weight // jnp.sum(weight, 1, keepdims=True)
    seq_lengths = MIN_LEN + share_tok
    seq_lengths = seq_lengths.at[:, 0].add(filled - jnp.sum(seq_lengths, 1))
    return seq_lengths.reshape(MICRO, NSEQ).astype(jnp.int32)


def block_levels(key, dims, cuts, smallest, largest):
    gain, own = 1.0, jax.random.fold_in(key, 6)
    for dim, parts in cuts:
        steps = jnp.exp(jax.random.uniform(jax.random.fold_in(own, dim), (parts,), jnp.float32, smallest / len(cuts), largest / len(cuts)))
        gain = gain * jnp.repeat(steps, dims[dim] // parts).reshape([-1 if axis == dim else 1 for axis in range(len(dims))])
    return gain


def normal_values(rng, dims, deviation, reach, cuts=(), kind=jnp.bfloat16):
    values = deviation * jax.random.normal(rng, dims, jnp.float32)
    if cuts:
        values = values * block_levels(rng, dims, cuts, -0.22, 0.18)
    return jnp.clip(values, -reach, reach).astype(kind)


def setup_inputs(seed: int = 0) -> dict:
    arg_keys = jax.random.split(jax.random.key(seed), 12)
    return {
        "tokens": normal_values(arg_keys[0], (MICRO, TOKENS, D), 1.0, 6.0, ((1, 32),)),
        "lengths": draw_lengths(jax.random.fold_in(arg_keys[11], 71), 0),
        "pairing": jax.vmap(lambda own: jax.random.permutation(own, QUESTION_COUNT))(jax.random.split(arg_keys[2], MICRO)).reshape((MICRO, QUESTION_COUNT)).astype(jnp.int32),
        "w_qkv": normal_values(arg_keys[3], (D, 3 * D), D ** -0.5, 0.21875),
        "w_out": normal_values(arg_keys[4], (D, D), (D // 16) ** -0.5, 0.875),
        "w_gate_up": normal_values(arg_keys[5], (D, 2 * FF), D ** -0.5, 0.21875),
        "w_down": normal_values(arg_keys[6], (FF, D), FF ** -0.5, 0.109375),
        "norm1_gain": jnp.clip(1.0 + 0.1 * jax.random.normal(arg_keys[7], (D,), jnp.float32), 0.5, 1.5),
        "norm1_bias": normal_values(arg_keys[8], (D,), 0.1, 0.6, (), jnp.float32),
        "norm2_gain": jnp.clip(1.0 + 0.1 * jax.random.normal(arg_keys[9], (D,), jnp.float32), 0.5, 1.5),
        "norm2_bias": normal_values(arg_keys[10], (D,), 0.1, 0.6, (), jnp.float32),
    }


highest_score_entry = lax.Precision.HIGHEST
sharpness_divisor = 0.02
loss_factor = 32.0
rope_base = 1000.0
norm_eps = 1e-05
unit_eps = 1e-06

@jax.custom_vjp
def low(v):
    return lax.optimization_barrier(v.astype(jnp.bfloat16)).astype(jnp.float32)

@jax.custom_vjp
def low_back(v):
    return v

def low_keep(v):
    return (low(v), None)

def low_pass(kept, grad):
    return (grad,)

def retained_for_reverse(v):
    return (v, None)

def back_low(kept, grad):
    return (low(grad),)
low.defvjp(low_keep, low_pass)
low_back.defvjp(retained_for_reverse, back_low)

def layout(seq_lengths):
    seq_lengths = seq_lengths.astype(jnp.int32)
    starts = (jnp.cumsum(seq_lengths) - seq_lengths).astype(jnp.int32)
    tok_index = jnp.arange(TOK_DEV).astype(jnp.int32)
    inside = (tok_index[:, None] >= starts[None, :]) & (tok_index[:, None] < (starts + seq_lengths)[None, :])
    slot_ids = jnp.arange(SEQ_DEV).astype(jnp.int32)
    is_live = jnp.any(inside, 1)
    segment = lax.optimization_barrier(jnp.sum(jnp.where(inside, slot_ids[None, :], 0), 1)).astype(jnp.int32) + jnp.where(is_live, 0, SEQ_DEV).astype(jnp.int32)
    position = tok_index - lax.optimization_barrier(jnp.sum(jnp.where(inside, starts[None, :], 0), 1)).astype(jnp.int32)
    return (inside.astype(jnp.float32), segment, position)

def rope_tables(position):
    half_dim = HEAD_DIM // 2
    freq = jnp.exp(jnp.arange(half_dim).astype(jnp.float32) * (-2.0 * math.log(rope_base) / HEAD_DIM))
    angle = position.astype(jnp.float32)[:, None] * freq[None, :]
    return (jnp.cos(angle)[:, None, :], jnp.sin(angle)[:, None, :])

def rotate(values, cosine, sine):
    half_dim = HEAD_DIM // 2
    first = values[..., :half_dim]
    second = values[..., half_dim:]
    return jnp.concatenate([first * cosine - second * sine, second * cosine + first * sine], -1)

def layer_norm(resid, gain_vec, bias_vec):
    row_mean = lax.optimization_barrier(jnp.mean(resid, -1, keepdims=True))
    centered = resid - row_mean
    variance = lax.optimization_barrier(jnp.mean(centered * centered, -1, keepdims=True))
    return centered * lax.rsqrt(variance + norm_eps) * gain_vec + bias_vec

def block(inputs, seq_lengths, w_qkv, w_out, w_gate_up, w_down, gain_one, bias_one, gain_two, bias_two):
    member, segment, position = layout(seq_lengths)
    cosine, sine = rope_tables(position)
    qkv_proj = low_back(jnp.dot(inputs, w_qkv, precision=highest_score_entry))
    shape_heads = (TOK_DEV, HEADS, HEAD_DIM)
    q_rot = low(rotate(qkv_proj[:, :D].reshape(shape_heads), cosine, sine))
    k_rot = low(rotate(qkv_proj[:, D:2 * D].reshape(shape_heads), cosine, sine))
    v_low = low(qkv_proj[:, 2 * D:].reshape(shape_heads))
    raw_scores = low_back(jnp.einsum('thd,shd->hts', q_rot, k_rot, precision=highest_score_entry))
    allowed = (segment[:, None] == segment[None, :])[None]
    scores = jnp.where(allowed, raw_scores * 0.125, -1e+30)
    prob_rows = jax.nn.softmax(scores, axis=-1)
    attended = jnp.einsum('hts,shd->thd', low(prob_rows), v_low, precision=highest_score_entry).reshape(TOK_DEV, D)
    attended = low_back(low(attended))
    attn_proj = low_back(jnp.dot(attended, w_out, precision=highest_score_entry))
    normed_one = layer_norm(inputs + attn_proj, gain_one, bias_one)
    gate_up = low_back(jnp.dot(low(normed_one), w_gate_up, precision=highest_score_entry))
    hidden_act = low(jax.nn.silu(gate_up[:, :FF]) * gate_up[:, FF:])
    mlp_out = low_back(jnp.dot(hidden_act, w_down, precision=highest_score_entry))
    outputs = layer_norm(normed_one + mlp_out, gain_two, bias_two)
    pooled = jnp.einsum('tk,td->kd', member, outputs, precision=highest_score_entry) / seq_lengths.astype(jnp.float32)[:, None]
    return (outputs, pooled)

def contrast(pooled, pairs):
    encoded_passages = pooled * lax.rsqrt(lax.optimization_barrier(jnp.sum(pooled * pooled, -1, keepdims=True)) + unit_eps)
    pairwise_affinity_matrix = jnp.einsum('aj,vj->av', encoded_passages[:QUESTION_COUNT], encoded_passages[QUESTION_COUNT:], precision=highest_score_entry) / sharpness_divisor
    log_total = jax.scipy.special.logsumexp(pairwise_affinity_matrix, axis=-1)
    chosen = jnp.take_along_axis(pairwise_affinity_matrix, pairs.astype(jnp.int32)[:, None], axis=1)[:, 0]
    cross = log_total - chosen
    return (loss_factor * jnp.sum(cross), jnp.mean(cross))

def reference(tokens, lengths, pairing, w_qkv, w_out, w_gate_up, w_down, norm1_gain, norm1_bias, norm2_gain, norm2_bias):
    weights = tuple((array_in.astype(jnp.float32) for array_in in (w_qkv, w_out, w_gate_up, w_down, norm1_gain, norm1_bias, norm2_gain, norm2_bias)))
    totals = tuple((jnp.zeros_like(array_in) for array_in in weights))
    loss_list = []
    act_list = []
    dx_list = []
    for micro_step in range(MICRO):
        device_tokens = tokens[micro_step].astype(jnp.float32).reshape(N_DP, TOK_DEV, D)
        device_lengths = lengths[micro_step].reshape(N_DP, SEQ_DEV)
        pairs = pairing[micro_step]

        def forward(token_blocks, *params):

            def one_device(pair_in):
                return block(pair_in[0], pair_in[1], *params)
            outputs, pooled = lax.map(jax.checkpoint(one_device), (token_blocks, device_lengths))
            objective, mean_loss = contrast(pooled.reshape(NSEQ, D), pairs)
            return (objective, (outputs, mean_loss))
        objective, pull_back, aux_out = jax.vjp(forward, device_tokens, *weights, has_aux=True)
        grads = pull_back(jnp.ones_like(objective))
        loss_list.append(aux_out[1])
        act_list.append(aux_out[0].reshape(TOKENS, D))
        dx_list.append(grads[0].reshape(TOKENS, D))
        totals = tuple((total + part for total, part in zip(totals, grads[1:])))
    return (jnp.stack(loss_list), jnp.stack(act_list).astype(jnp.bfloat16), jnp.stack(dx_list), totals[0], totals[1], totals[2], totals[3], totals[4], totals[5], totals[6], totals[7])
```

```python
import math

import jax
import jax.numpy as jnp
from jax import lax
from jax.sharding import PartitionSpec as P

HEAD_DIM = 64
HIGH = lax.Precision.HIGHEST
SHARPNESS = 0.02
LOSS_FACTOR = 32.0
ROPE_BASE = 1000.0
NORM_EPS = 1e-05
UNIT_EPS = 1e-06


def layout(seq_lengths, rows):
    slots = seq_lengths.shape[0]
    index = jnp.arange(rows, dtype=jnp.int32)
    start = jnp.int32(0)
    segment = jnp.full((rows,), slots, jnp.int32)
    position = index
    member = []
    for k in range(slots):
        end = start + seq_lengths[k]
        inside = (index >= start) & (index < end)
        segment = jnp.where(inside, k, segment)
        position = jnp.where(inside, index - start, position)
        member.append(inside.astype(jnp.float32))
        start = end
    return jnp.stack(member, 1), segment, position


def rope_tables(position):
    half = HEAD_DIM // 2
    freq = jnp.exp(
        jnp.arange(half).astype(jnp.float32) * (-2.0 * math.log(ROPE_BASE) / HEAD_DIM)
    )
    angle = position.astype(jnp.float32)[:, None] * freq[None, :]
    return jnp.cos(angle)[:, None, :], jnp.sin(angle)[:, None, :]


def rotate(values, cosine, sine):
    first, second = jnp.split(values, 2, -1)
    return jnp.concatenate([first * cosine - second * sine, second * cosine + first * sine], -1)


def unrotate(grad, cosine, sine):
    return rotate(grad, cosine, -sine)


def norm_forward(resid, gain, bias):
    centered = resid - jnp.mean(resid, -1, keepdims=True)
    inv_std = lax.rsqrt(jnp.mean(centered * centered, -1, keepdims=True) + NORM_EPS)
    unit = centered * inv_std
    return unit * gain + bias, unit, inv_std


def norm_back(grad, unit, inv_std, gain):
    scaled = grad * gain
    back = inv_std * (
        scaled
        - jnp.mean(scaled, -1, keepdims=True)
        - unit * jnp.mean(scaled * unit, -1, keepdims=True)
    )
    return back, jnp.sum(grad * unit, 0), jnp.sum(grad, 0)


def contrast(everyone, pairing, first_row, own_rows):
    queries = everyone.shape[0] // 2
    question, document = everyone[:queries], everyone[queries:]
    logits = jnp.einsum("ad,bd->ab", question, document, precision=HIGH) / SHARPNESS
    top = jnp.max(logits, -1, keepdims=True)
    log_total = top + jnp.log(jnp.sum(jnp.exp(logits - top), -1, keepdims=True))
    target = (pairing[:, None] == jnp.arange(queries)[None, :]).astype(jnp.float32)
    loss = jnp.sum(log_total[:, 0] - jnp.sum(logits * target, 1)) / queries
    d_logits = LOSS_FACTOR * (jnp.exp(logits - log_total) - target) / SHARPNESS
    d_everyone = jnp.concatenate(
        [
            jnp.einsum("ab,bd->ad", d_logits, document, precision=HIGH),
            jnp.einsum("ab,ad->bd", d_logits, question, precision=HIGH),
        ],
        0,
    )
    return loss, lax.dynamic_slice_in_dim(d_everyone, first_row, own_rows, 0)


def at(array, index):
    return lax.dynamic_index_in_dim(array, index, 1, keepdims=False)


def scatter_sum(grad, count):
    me = lax.axis_index("dp")
    rows, columns = grad.shape
    core, low, high = me & 1, (me >> 1) & 1, (me >> 2) & 1
    outer = count // 8

    def swap(array, even_bit, odd_bit):
        pairs = [(i, i ^ (1 << (odd_bit if i & 1 else even_bit))) for i in range(count)]
        return lax.ppermute(array, "dp", pairs)

    blocks = grad.reshape(outer * 4, 2, rows // count, columns)
    keep = at(blocks, core).reshape(outer, 4, rows // count, columns)
    got_core = swap(at(blocks, 1 - core), 0, 0).reshape(keep.shape)

    def place(first, second):
        return jnp.where(core == 0, second * 2 + first, first * 2 + second)

    mine_first, mine_second = jnp.where(core == 0, low, high), jnp.where(core == 0, high, low)
    sent = jnp.stack(
        [at(keep, place(1 - mine_first, j)) + at(got_core, place(1 - mine_first, j)) for j in range(2)], 1
    )
    got_first = swap(sent, 1, 2)
    other = place(mine_first, 1 - mine_second)
    got_second = swap(at(keep, other) + at(got_core, other) + at(got_first, 1 - mine_second), 2, 1)
    own = place(mine_first, mine_second)
    terms = [at(keep, own), at(got_core, own), at(got_first, mine_second), got_second]
    bit = count.bit_length() - 2
    while outer > 1:
        outer //= 2
        upper = (me >> bit) & 1
        half = lambda array, which: lax.dynamic_slice_in_dim(array, which * outer, outer, 0)
        sent = sum(half(t, 1 - upper) for t in terms)
        terms = [half(t, upper) for t in terms] + [swap(sent, bit, bit)]
        bit -= 1
    return sum(terms).reshape(rows // count, columns)


def body(
    tokens,
    lengths,
    pairing,
    w_qkv,
    w_out,
    w_gate_up,
    w_down,
    norm1_gain,
    norm1_bias,
    norm2_gain,
    norm2_bias,
):
    micro, rows, width = tokens.shape
    slots = lengths.shape[1]
    hidden = w_down.shape[0]
    heads = width // HEAD_DIM
    count = lax.axis_size("dp")
    me = lax.axis_index("dp")
    all_rows = micro * rows
    split = (micro, rows, heads, HEAD_DIM)

    member, segment, position = jax.vmap(lambda own: layout(own, rows))(lengths)
    cosine, sine = jax.vmap(rope_tables)(position)
    allowed = (segment[:, :, None] == segment[:, None, :])[:, None]
    flat = tokens.reshape(all_rows, width)
    qkv = jnp.dot(flat, w_qkv, preferred_element_type=jnp.float32)
    q, k, v = (qkv[:, i * width : (i + 1) * width].reshape(split) for i in range(3))
    q = rotate(q, cosine, sine).astype(jnp.bfloat16)
    k = rotate(k, cosine, sine).astype(jnp.bfloat16)
    v = v.astype(jnp.bfloat16)
    scores = jnp.einsum("bthd,bshd->bhts", q, k, preferred_element_type=jnp.float32)
    scores = jnp.where(allowed, scores * 0.125, -1e30)
    top = jnp.max(scores, -1, keepdims=True)
    total = jnp.sum(jnp.exp(scores - top), -1, keepdims=True)
    log_total = top + jnp.log(total)
    probs = jnp.exp(scores - log_total).astype(jnp.bfloat16)
    attended = jnp.einsum("bhts,bshd->bthd", probs, v, preferred_element_type=jnp.float32)
    attended = attended.reshape(all_rows, width).astype(jnp.bfloat16)
    attn = jnp.dot(attended, w_out, preferred_element_type=jnp.float32)
    normed, unit_one, inv_one = norm_forward(flat.astype(jnp.float32) + attn, norm1_gain, norm1_bias)
    normed_low = normed.astype(jnp.bfloat16)
    gate_up = jnp.dot(normed_low, w_gate_up, preferred_element_type=jnp.float32)
    gate, up = gate_up[:, :hidden], gate_up[:, hidden:]
    act = (jax.nn.silu(gate) * up).astype(jnp.bfloat16)
    mlp = jnp.dot(act, w_down, preferred_element_type=jnp.float32)
    outputs, unit_two, inv_two = norm_forward(normed + mlp, norm2_gain, norm2_bias)

    length = lengths.astype(jnp.float32)[:, :, None]
    pooled = (
        jnp.einsum("btk,btd->bkd", member, outputs.reshape(micro, rows, width), precision=HIGH) / length
    )
    inv_norm = lax.rsqrt(jnp.sum(pooled * pooled, -1, keepdims=True) + UNIT_EPS)
    embed = pooled * inv_norm
    gathered = lax.all_gather(embed, "dp", axis=1, tiled=True)
    losses, d_embed = [], []
    for b in range(micro):
        loss, own = contrast(gathered[b], pairing[b], me * slots, slots)
        losses.append(loss)
        d_embed.append(own)
    d_embed = jnp.stack(d_embed)
    d_pooled = inv_norm * (d_embed - embed * jnp.sum(d_embed * embed, -1, keepdims=True))
    d_outputs = jnp.einsum("btk,bkd->btd", member, d_pooled / length, precision=HIGH)
    d_outputs = d_outputs.reshape(all_rows, width)

    d_two, d_gain_two, d_bias_two = norm_back(d_outputs, unit_two, inv_two, norm2_gain)
    d_mlp = d_two.astype(jnp.bfloat16)
    g_down = jnp.einsum("tf,td->fd", act, d_mlp, preferred_element_type=jnp.float32)
    g_down = scatter_sum(g_down, count)
    d_hidden = jnp.einsum("td,fd->tf", d_mlp, w_down, preferred_element_type=jnp.float32)
    sig = jax.nn.sigmoid(gate)
    d_gate = d_hidden * up * sig * (1.0 + gate * (1.0 - sig))
    d_up = d_hidden * gate * sig
    d_gate_up = jnp.concatenate([d_gate, d_up], 1).astype(jnp.bfloat16)
    g_gate_up = jnp.einsum("td,tf->df", normed_low, d_gate_up, preferred_element_type=jnp.float32)
    g_gate_up = scatter_sum(g_gate_up, count)
    d_normed = d_two + jnp.einsum("tf,df->td", d_gate_up, w_gate_up, preferred_element_type=jnp.float32)
    d_one, d_gain_one, d_bias_one = norm_back(d_normed, unit_one, inv_one, norm1_gain)
    d_proj = d_one.astype(jnp.bfloat16)
    g_out = jnp.einsum("ti,to->io", attended, d_proj, preferred_element_type=jnp.float32)
    d_attended = jnp.einsum("to,io->ti", d_proj, w_out, preferred_element_type=jnp.float32)
    d_attended = d_attended.astype(jnp.bfloat16).reshape(split)

    scores = jnp.einsum("bthd,bshd->bhts", q, k, preferred_element_type=jnp.float32)
    probs = jnp.exp(jnp.where(allowed, scores * 0.125, -1e30) - log_total)
    d_probs = jnp.einsum("bthd,bshd->bhts", d_attended, v, preferred_element_type=jnp.float32)
    delta = jnp.sum(probs * d_probs, -1, keepdims=True)
    d_scores = (probs * (d_probs - delta) * 0.125).astype(jnp.bfloat16)
    d_q = jnp.einsum("bhts,bshd->bthd", d_scores, k, preferred_element_type=jnp.float32)
    d_k = jnp.einsum("bhts,bthd->bshd", d_scores, q, preferred_element_type=jnp.float32)
    d_v = jnp.einsum(
        "bhts,bthd->bshd", probs.astype(jnp.bfloat16), d_attended, preferred_element_type=jnp.float32
    )
    d_qkv = jnp.concatenate(
        [
            part.reshape(all_rows, width)
            for part in (rotate(d_q, cosine, -sine), rotate(d_k, cosine, -sine), d_v)
        ],
        1,
    ).astype(jnp.bfloat16)
    g_qkv = jnp.einsum("ti,to->io", flat, d_qkv, preferred_element_type=jnp.float32)
    g_qkv = scatter_sum(jnp.concatenate([g_qkv, g_out], 1), count)
    d_tokens = d_one + jnp.einsum("to,io->ti", d_qkv, w_qkv, preferred_element_type=jnp.float32)
    norms = jnp.stack([d_gain_one, d_bias_one, d_gain_two, d_bias_two])
    norms = lax.psum_scatter(norms, "dp", scatter_dimension=1, tiled=True)
    return (
        jnp.stack(losses),
        outputs.reshape(tokens.shape).astype(jnp.bfloat16),
        d_tokens.reshape(tokens.shape),
        g_qkv[:, : 3 * width],
        g_qkv[:, 3 * width :],
        g_gate_up,
        g_down,
        norms[0],
        norms[1],
        norms[2],
        norms[3],
    )


def solution(mesh):
    tokens, rows = P(None, "dp", None), P("dp", None)
    return jax.shard_map(
        body,
        mesh=mesh,
        in_specs=(tokens, P(None, "dp"), P(), P(), P(), P(), P(), P(), P(), P(), P()),
        out_specs=(P(), tokens, tokens, rows, rows, rows, rows, P("dp"), P("dp"), P("dp"), P("dp")),
        check_vma=False,
    )
```

```python
import functools
import math

import jax
import jax.numpy as jnp
from jax import lax
from jax.experimental import pallas as pl
from jax.experimental.pallas import tpu as pltpu
from jax.sharding import PartitionSpec as P

HEAD_DIM = 64
LANES = 128
BLOCK = 128
TILE = 256
HIGH = lax.Precision.HIGHEST
SHARPNESS = 0.02
LOSS_FACTOR = 32.0
ROPE_BASE = 1000.0
NORM_EPS = 1e-05
UNIT_EPS = 1e-06
MASKED = -1e30
VMEM = 60 * 2**20
F32, BF16 = jnp.float32, jnp.bfloat16


def dot(a, b, contract=(1, 0)):
    return lax.dot_general(a, b, (((contract[0],), (contract[1],)), ((), ())), preferred_element_type=F32)


def lane_of(shape):
    return lax.broadcasted_iota(jnp.int32, shape, len(shape) - 1)


def params(*semantics):
    return pltpu.CompilerParams(
        dimension_semantics=semantics or None, vmem_limit_bytes=VMEM
    )


def segment_of(index, ends_ref, batch, slots):
    segment = jnp.zeros_like(index)
    for k in range(slots):
        segment += (index >= ends_ref[batch, k]).astype(jnp.int32)
    return segment


def turned(values, cosine, sine):
    low = (lane_of(values.shape) & (HEAD_DIM // 2)) == 0
    other = jnp.where(
        low, pltpu.roll(values, LANES - HEAD_DIM // 2, 1), pltpu.roll(values, HEAD_DIM // 2, 1)
    )
    return values * cosine + other * sine


def sigmoid(x):
    return 0.5 * jnp.tanh(0.5 * x) + 0.5


def thirds(x):
    top = x.astype(BF16)
    rest = x - top.astype(F32)
    middle = rest.astype(BF16)
    return top, middle, (rest - middle.astype(F32)).astype(BF16)


def with_extras(own, main, extra):
    place = lane_of(main.shape) & (HEAD_DIM - 1)
    top, middle, last = thirds(-extra)
    zero = jnp.zeros_like(main)
    rest = jnp.where(place == 0, top, jnp.where(place == 1, middle, jnp.where(place == 2, last, zero)))
    return jnp.where(own, main, rest)


def qkv_kernel(x_ref, w_ref, cos_ref, sin_ref, out_ref):
    width = x_ref.shape[1]
    x = x_ref[...]
    cosine, sine = cos_ref[...], sin_ref[...]
    for c in range(0, 3 * width, TILE):
        y = dot(x, w_ref[:, c : c + TILE])
        for half in range(0, TILE, LANES):
            part = y[:, half : half + LANES]
            if c < 2 * width:
                part = turned(part, cosine, sine)
            out_ref[:, c + half : c + half + LANES] = part.astype(BF16)


def project(x, w, cosine, sine):
    rows, width = x.shape
    return pl.pallas_call(
        qkv_kernel,
        grid=(rows // TILE,),
        in_specs=[
            pl.BlockSpec((TILE, width), lambda i: (i, 0)),
            pl.BlockSpec((width, 3 * width), lambda i: (0, 0), pipeline_mode=pl.Buffered(1)),
            pl.BlockSpec((TILE, LANES), lambda i: (i, 0)),
            pl.BlockSpec((TILE, LANES), lambda i: (i, 0)),
        ],
        out_specs=pl.BlockSpec((TILE, 3 * width), lambda i: (i, 0)),
        out_shape=jax.ShapeDtypeStruct((rows, 3 * width), BF16),
        compiler_params=params("arbitrary"),
        cost_estimate=pl.CostEstimate(
            flops=6 * rows * width * width, bytes_accessed=8 * rows * width + 6 * width * width, transcendentals=0
        ),
        name="qkv",
    )(x, w, cosine, sine)


def attend_kernel(
    ends_ref, start_ref, count_ref, q_ref, k_ref, v_ref, x_ref, w_ref, gain_ref, bias_ref,
    attended_ref, query_ref, unit_ref, inv_ref, low_ref, low_t_ref, mask_ref,
):
    batch, i = pl.program_id(0), pl.program_id(1)
    slots = ends_ref.shape[1]
    blocks = k_ref.shape[0] // BLOCK
    width = x_ref.shape[1]
    own_low = lane_of((BLOCK, LANES)) < HEAD_DIM
    start = start_ref[batch, i]

    def run(n):
        span = n * BLOCK
        rows_at = pl.multiple_of(start * BLOCK, BLOCK)
        row = lax.broadcasted_iota(jnp.int32, (BLOCK, LANES), 0) + i * BLOCK
        row_segment = segment_of(row, ends_ref, batch, slots)
        for j in range(n):
            column = lane_of((BLOCK, LANES)) + (rows_at + j * BLOCK)
            same = row_segment == segment_of(column, ends_ref, batch, slots)
            mask_ref[:, j * BLOCK : (j + 1) * BLOCK] = jnp.where(same, 0.0, MASKED)

        def pair(p, _):
            at = pl.ds(pl.multiple_of(p * LANES, LANES), LANES)
            q = q_ref[:, at]
            k = k_ref[pl.ds(rows_at, span), at]
            v = v_ref[pl.ds(rows_at, span), at]
            scaled = q * jnp.asarray(0.125, BF16)
            wide_low = lane_of((span, LANES)) < HEAD_DIM
            parts = []
            for h in range(2):
                own = own_low if h == 0 else ~own_low
                wide = wide_low if h == 0 else ~wide_low
                scores = dot(jnp.where(own, scaled, jnp.zeros_like(q)), k, (1, 1))
                scores = scores + mask_ref[:, :span]
                top = jnp.max(scores, -1, keepdims=True)
                probs = jnp.exp(scores - top).astype(BF16)
                mixed = dot(probs, jnp.where(wide, v, jnp.ones_like(v)))
                total = pltpu.roll(mixed, HEAD_DIM, 1)
                parts.append(mixed / total)
                query_ref[:, pl.ds(pl.multiple_of((2 * p + h) * LANES, LANES), LANES)] = with_extras(
                    own, scaled, top + jnp.log(mixed)
                )
            attended_ref[:, at] = jnp.where(own_low, parts[0], parts[1]).astype(BF16)
            return 0

        lax.fori_loop(0, width // LANES, pair, 0)

    for n in range(1, blocks + 1):
        pl.when(count_ref[batch, i] == n)(functools.partial(run, n))

    resid = x_ref[...].astype(F32) + dot(attended_ref[...], w_ref[...])
    centered = resid - jnp.mean(resid, -1, keepdims=True)
    inv = lax.rsqrt(jnp.mean(centered * centered, -1, keepdims=True) + NORM_EPS)
    unit = centered * inv
    unit_ref[...] = unit
    inv_ref[...] = jnp.broadcast_to(inv, inv_ref.shape)
    low = (unit * gain_ref[...] + bias_ref[...]).astype(BF16)
    low_ref[...] = low
    low_t_ref[...] = low.T


def attend(ends, starts, counts, qkv, x, w_out, gain, bias):
    rows, width = x.shape
    batches = ends.shape[0]
    per = rows // batches
    blocks = per // BLOCK
    row = lambda columns: pl.BlockSpec((BLOCK, columns), lambda b, i, *_: (b * blocks + i, 0))
    whole = lambda c: pl.BlockSpec((per, width), lambda b, i, *_: (b, c))
    fixed = lambda *shape: pl.BlockSpec(shape, lambda b, i, *_: (0, 0))
    wide = 2 * width
    return pl.pallas_call(
        attend_kernel,
        grid_spec=pltpu.PrefetchScalarGridSpec(
            num_scalar_prefetch=3,
            grid=(batches, blocks),
            in_specs=[row(width), whole(1), whole(2), row(width), fixed(width, width), fixed(1, width), fixed(1, width)],
            out_specs=[
                row(width), row(wide), row(width), row(LANES), row(width),
                pl.BlockSpec((width, BLOCK), lambda b, i, *_: (0, b * blocks + i)),
            ],
            scratch_shapes=[pltpu.VMEM((BLOCK, per), F32)],
        ),
        out_shape=[
            jax.ShapeDtypeStruct((rows, width), BF16),
            jax.ShapeDtypeStruct((rows, wide), BF16),
            jax.ShapeDtypeStruct((rows, width), F32),
            jax.ShapeDtypeStruct((rows, LANES), F32),
            jax.ShapeDtypeStruct((rows, width), BF16),
            jax.ShapeDtypeStruct((width, rows), BF16),
        ],
        compiler_params=params("arbitrary", "arbitrary"),
        cost_estimate=pl.CostEstimate(
            flops=12 * rows * per * width, bytes_accessed=30 * rows * width, transcendentals=rows * per * 12
        ),
        name="attend",
    )(ends, starts, counts, qkv, qkv, qkv, x, w_out, gain, bias)


def mlp_kernel(
    ends_ref, unit1_ref, low_ref, wgu_ref, wd_ref, gain1_ref, bias1_ref, gain2_ref, bias2_ref,
    gate_ref, up_ref, act_ref, unit_ref, inv_ref, out_ref, pool_ref,
):
    i = pl.program_id(0)
    batches, slots = ends_ref.shape
    hidden = wd_ref.shape[0]
    per = pl.num_programs(0) // batches
    low = low_ref[...]
    step = 2 * TILE
    total = None
    for c in range(0, hidden, step):
        gate = dot(low, wgu_ref[:, c : c + step])
        up = dot(low, wgu_ref[:, hidden + c : hidden + c + step])
        act = (gate * sigmoid(gate) * up).astype(BF16)
        gate_ref[:, c : c + step] = gate.astype(BF16)
        up_ref[:, c : c + step] = up.astype(BF16)
        act_ref[:, c : c + step] = act
        part = dot(act, wd_ref[c : c + step, :])
        total = part if total is None else total + part
    resid = unit1_ref[...] * gain1_ref[...] + bias1_ref[...] + total
    centered = resid - jnp.mean(resid, -1, keepdims=True)
    inv = lax.rsqrt(jnp.mean(centered * centered, -1, keepdims=True) + NORM_EPS)
    unit = centered * inv
    unit_ref[...] = unit
    inv_ref[...] = jnp.broadcast_to(inv, inv_ref.shape)
    out = unit * gain2_ref[...] + bias2_ref[...]
    out_ref[...] = out.astype(BF16)
    row = lax.broadcasted_iota(jnp.int32, (TILE, 1), 0) + (i % per) * TILE
    segment = segment_of(row, ends_ref, i // per, slots)

    @pl.when(i % per == 0)
    def _():
        pool_ref[...] = jnp.zeros_like(pool_ref)

    for k in range(slots):
        pool_ref[0, k : k + 1, :] += jnp.sum(jnp.where(segment == k, out, 0.0), 0, keepdims=True)


def feed_forward(ends, unit_one, low, w_gate_up, w_down, gain1, bias1, gain2, bias2):
    rows, width = low.shape
    hidden = w_down.shape[0]
    batches, slots = ends.shape
    per = rows // batches // TILE
    row = lambda columns: pl.BlockSpec((TILE, columns), lambda i, *_: (i, 0))
    fixed = lambda *shape: pl.BlockSpec(shape, lambda i, *_: (0, 0), pipeline_mode=pl.Buffered(1))
    return pl.pallas_call(
        mlp_kernel,
        grid_spec=pltpu.PrefetchScalarGridSpec(
            num_scalar_prefetch=1,
            grid=(rows // TILE,),
            in_specs=[row(width), row(width), fixed(width, 2 * hidden), fixed(hidden, width)] + [fixed(1, width)] * 4,
            out_specs=[
                row(hidden), row(hidden), row(hidden), row(width), row(LANES), row(width),
                pl.BlockSpec((1, slots, width), lambda i, *_: (i // per, 0, 0)),
            ],
        ),
        out_shape=[
            jax.ShapeDtypeStruct((rows, hidden), BF16),
            jax.ShapeDtypeStruct((rows, hidden), BF16),
            jax.ShapeDtypeStruct((rows, hidden), BF16),
            jax.ShapeDtypeStruct((rows, width), F32),
            jax.ShapeDtypeStruct((rows, LANES), F32),
            jax.ShapeDtypeStruct((rows, width), BF16),
            jax.ShapeDtypeStruct((batches, slots, width), F32),
        ],
        compiler_params=params("arbitrary"),
        cost_estimate=pl.CostEstimate(
            flops=6 * rows * width * hidden,
            bytes_accessed=6 * rows * hidden + 6 * width * hidden + 12 * rows * width,
            transcendentals=rows * hidden,
        ),
        name="feed_forward",
    )(ends, unit_one, low, w_gate_up, w_down, gain1, bias1, gain2, bias2)


def stage_bits(count):
    far = [(b, b) for b in range(count.bit_length() - 2, 2, -1)]
    return far + [(2, 1), (1, 2), (0, 0)]


def contrast_kernel(
    count, slots, pool_ref, length_ref, pair_ref, back_ref, loss_ref, held, every, d_rows, d_columns, send_sem, recv_sem
):
    me = lax.axis_index("dp")
    core = lax.rem(me, 2)
    own, width = pool_ref.shape
    batches = own // slots
    bits = stage_bits(count)
    flips = [jnp.where(core == 0, 1 << even, 1 << odd) for even, odd in bits]
    length = length_ref[...]
    pooled = pool_ref[...] / length
    inv = lax.rsqrt(jnp.sum(pooled * pooled, -1, keepdims=True) + UNIT_EPS)
    embed = pooled * inv
    held[0] = embed

    barrier = pltpu.get_barrier_semaphore()
    for flip in flips:
        pl.semaphore_signal(
            barrier, inc=1, device_id=(me ^ flip,), device_id_type=pl.DeviceIdType.MESH
        )
    pl.semaphore_wait(barrier, len(bits))
    for k, flip in enumerate(flips):
        size = 1 << k
        copy = pltpu.make_async_remote_copy(
            src_ref=held.at[pl.ds(0, size)],
            dst_ref=held.at[pl.ds(size, size)],
            send_sem=send_sem.at[k],
            recv_sem=recv_sem.at[k],
            device_id=(me ^ flip,),
            device_id_type=pl.DeviceIdType.MESH,
        )
        copy.start()
        copy.wait()

    for s in range(count):
        even = sum(1 << bits[k][0] for k in range(len(bits)) if s >> k & 1)
        odd = sum(1 << bits[k][1] for k in range(len(bits)) if s >> k & 1)
        crossed = s >> (len(bits) - 1)
        device = me ^ jnp.where((core ^ crossed) == 0, even, odd)
        every[pl.ds(pl.multiple_of(device * own, own), own), :] = held[s]

    half = count // 2 * own
    questions, documents = every[:half, :], every[half:, :]
    exact = functools.partial(lax.dot_general, precision=HIGH, preferred_element_type=F32)
    logits = exact(questions, documents, (((1,), (1,)), ((), ()))) / SHARPNESS
    row = lax.broadcasted_iota(jnp.int32, (half, half), 0)
    column = lax.broadcasted_iota(jnp.int32, (half, half), 1)
    same = ((row // slots) % batches) == ((column // slots) % batches)
    logits = jnp.where(same, logits, MASKED)
    top = jnp.max(logits, -1, keepdims=True)
    log_total = top + jnp.log(jnp.sum(jnp.exp(logits - top), -1, keepdims=True))
    document = (column // own) * slots + column % slots
    target = same & (document == pair_ref[...])
    cross = log_total - jnp.sum(jnp.where(target, logits, 0.0), -1, keepdims=True)
    batch = (lax.broadcasted_iota(jnp.int32, (half, 1), 0) // slots) % batches
    lines = lax.broadcasted_iota(jnp.int32, loss_ref.shape, 0)
    losses = jnp.zeros(loss_ref.shape, F32)
    for b in range(batches):
        mean = jnp.sum(jnp.where(batch == b, cross, 0.0)) / (half // batches)
        losses = jnp.where(lines == b, mean, losses)
    loss_ref[...] = losses
    d_logits = LOSS_FACTOR * (jnp.exp(logits - log_total) - target.astype(F32)) / SHARPNESS
    d_rows[...] = d_logits
    d_columns[...] = d_logits.T
    at = pl.ds(pl.multiple_of(lax.rem(me, count // 2) * own, own), own)
    d_question = exact(d_rows[at, :], documents, (((1,), (0,)), ((), ())))
    d_document = exact(d_columns[at, :], questions, (((1,), (0,)), ((), ())))
    d_embed = jnp.where(me < count // 2, d_question, d_document)
    back_ref[...] = inv * (d_embed - embed * jnp.sum(d_embed * embed, -1, keepdims=True)) / length


def contrast(count, pool, lengths, pairing):
    batches, slots, width = pool.shape
    own = batches * slots
    half = count // 2 * own
    pairs = pairing.reshape(batches, count // 2, slots).transpose(1, 0, 2).reshape(half, 1)
    stages = count.bit_length() - 1
    vmem = pl.BlockSpec(memory_space=pltpu.VMEM)
    back, losses = pl.pallas_call(
        functools.partial(contrast_kernel, count, slots),
        in_specs=[vmem] * 3,
        out_specs=[vmem] * 2,
        out_shape=[jax.ShapeDtypeStruct((own, width), F32), jax.ShapeDtypeStruct((8, LANES), F32)],
        scratch_shapes=[
            pltpu.VMEM((count, own, width), F32),
            pltpu.VMEM((count * own, width), F32),
            pltpu.VMEM((half, half), F32),
            pltpu.VMEM((half, half), F32),
            pltpu.SemaphoreType.DMA((stages,)),
            pltpu.SemaphoreType.DMA((stages,)),
        ],
        compiler_params=pltpu.CompilerParams(collective_id=0, has_side_effects=True, vmem_limit_bytes=VMEM),
        name="contrast",
    )(pool.reshape(own, width), lengths.reshape(own, 1).astype(F32), pairs)
    return losses[:batches, 0], back


def split_shapes(count, rows, columns):
    per = rows // count
    if per % 8:
        return [jax.ShapeDtypeStruct((rows, columns), F32)]
    return [jax.ShapeDtypeStruct((count // 2, per, columns), F32)] * 2


def split_specs(count, rows, columns, place):
    per = rows // count
    if per % 8:
        return [pl.BlockSpec((rows, columns), lambda *i: (0, place(*i)))]
    return [pl.BlockSpec((count // 2, per, columns), lambda *i: (0, 0, place(*i)))] * 2


def emit(result, first, refs, columns=slice(None)):
    if len(refs) == 1:
        refs[0][first : first + result.shape[0], columns] = result
        return
    keep, send = refs
    even_core = lax.rem(lax.axis_index("dp"), 2) == 0
    per = keep.shape[1]
    for m in range(0, result.shape[0], 2 * per):
        zero, one = result[m : m + per], result[m + per : m + 2 * per]
        chip = (first + m) // (2 * per)
        keep[chip, :, columns] = jnp.where(even_core, zero, one)
        send[chip, :, columns] = jnp.where(even_core, one, zero)


def down_kernel(ends_ref, unit_ref, inv_ref, back_ref, gain_ref, act_ref, two_ref, low_ref, sums_ref, *grads):
    rows, width = unit_ref.shape
    batches, slots = ends_ref.shape

    @pl.when(pl.program_id(0) == 0)
    def _():
        gain = gain_ref[...]
        gain_sum = bias_sum = jnp.zeros((1, width), F32)
        for t in range(0, rows, TILE):
            b = t * batches // rows
            index = lax.broadcasted_iota(jnp.int32, (TILE, 1), 0) + (t - b * (rows // batches))
            segment = segment_of(index, ends_ref, b, slots)
            grad = jnp.zeros((TILE, width), F32)
            for k in range(slots):
                grad = jnp.where(segment == k, back_ref[b * slots + k : b * slots + k + 1, :], grad)
            unit = unit_ref[t : t + TILE, :]
            scaled = grad * gain
            two = inv_ref[t : t + TILE, :1] * (
                scaled
                - jnp.mean(scaled, -1, keepdims=True)
                - unit * jnp.mean(scaled * unit, -1, keepdims=True)
            )
            two_ref[t : t + TILE, :] = two
            low_ref[t : t + TILE, :] = two.astype(BF16)
            gain_sum += jnp.sum(grad * unit, 0, keepdims=True)
            bias_sum += jnp.sum(grad, 0, keepdims=True)
        sums_ref[0:1, :] = gain_sum
        sums_ref[1:2, :] = bias_sum

    low = low_ref[...]
    step = 384
    for f in range(0, act_ref.shape[1], step):
        emit(dot(act_ref[:, f : f + step], low, (0, 0)), f, grads)


def down_back(count, ends, unit, inv, back, gain, act):
    rows, width = unit.shape
    hidden = act.shape[1]
    per = hidden // count
    tile = 768
    fixed = lambda *shape: pl.BlockSpec(shape, lambda i, *_: (0, 0), pipeline_mode=pl.Buffered(1))
    grad = pl.BlockSpec((tile // per // 2, per, width), lambda i, *_: (i, 0, 0))
    return pl.pallas_call(
        down_kernel,
        grid_spec=pltpu.PrefetchScalarGridSpec(
            num_scalar_prefetch=1,
            grid=(hidden // tile,),
            in_specs=[
                fixed(rows, width), fixed(rows, LANES), fixed(back.shape[0], width), fixed(1, width),
                pl.BlockSpec((rows, tile), lambda i, *_: (0, i)),
            ],
            out_specs=[fixed(rows, width), fixed(rows, width), fixed(8, width), grad, grad],
        ),
        out_shape=[
            jax.ShapeDtypeStruct((rows, width), F32),
            jax.ShapeDtypeStruct((rows, width), BF16),
            jax.ShapeDtypeStruct((8, width), F32),
        ]
        + split_shapes(count, hidden, width),
        compiler_params=params("arbitrary"),
        cost_estimate=pl.CostEstimate(
            flops=2 * rows * width * hidden, bytes_accessed=2 * rows * hidden + 4 * width * hidden + 10 * rows * width, transcendentals=0
        ),
        name="down_back",
    )(ends, unit, inv, back, gain, act)


def gate_kernel(low_ref, wd_ref, gate_ref, up_ref, normed_t_ref, wg_ref, wu_ref, sum_in_ref, sum_ref, *rest):
    *grads, pre_ref = rest
    width, rows = normed_t_ref.shape
    step = wd_ref.shape[0]

    @pl.when(pl.program_id(0) == 0)
    def _():
        sum_ref[...] = sum_in_ref[...]

    def tile(i, _):
        at = pl.ds(pl.multiple_of(i * TILE, TILE), TILE)
        d_hidden = dot(low_ref[at, :], wd_ref[...], (1, 1))
        gate = gate_ref[at, :].astype(F32)
        up = up_ref[at, :].astype(F32)
        sig = sigmoid(gate)
        silu = gate * sig
        d_gate = (d_hidden * up * (sig + silu * (1.0 - sig))).astype(BF16)
        d_up = (d_hidden * silu).astype(BF16)
        pre_ref[at, :step] = d_gate
        pre_ref[at, step:] = d_up
        sum_ref[at, :] += dot(d_gate, wg_ref[...], (1, 1)) + dot(d_up, wu_ref[...], (1, 1))
        return 0

    lax.fori_loop(0, rows // TILE, tile, 0)
    m = 192
    half = len(grads) // 2
    for r in range(0, width, m):
        left = normed_t_ref[r : r + m, :]
        for side in range(2):
            emit(dot(left, pre_ref[:, side * step : (side + 1) * step]), r, grads[side * half : (side + 1) * half])


def gate_back(count, part, parts, low, w_down, gate, up, normed_t, w_gate_up, total):
    rows, width = low.shape
    hidden = w_down.shape[0]
    step = 512
    steps = hidden // parts // step
    base = part * steps
    fixed = lambda *shape: pl.BlockSpec(shape, lambda i: (0, 0), pipeline_mode=pl.Buffered(1))
    column = lambda height, offset=0: pl.BlockSpec((height, step), lambda i: (0, offset + base + i))
    shapes = split_shapes(count, width, hidden // parts)
    specs = split_specs(count, width, step, lambda i: i)
    total, *grads = pl.pallas_call(
        gate_kernel,
        grid=(steps,),
        in_specs=[
            fixed(rows, width), pl.BlockSpec((step, width), lambda i: (base + i, 0)), column(rows), column(rows),
            fixed(width, rows), column(width), column(width, hidden // step), fixed(rows, width),
        ],
        out_specs=[fixed(rows, width)] + specs * 2,
        out_shape=[jax.ShapeDtypeStruct((rows, width), F32)] + shapes * 2,
        scratch_shapes=[pltpu.VMEM((rows, 2 * step), BF16)],
        compiler_params=params("arbitrary"),
        cost_estimate=pl.CostEstimate(
            flops=10 * rows * width * hidden // parts,
            bytes_accessed=(4 * rows * hidden + 14 * width * hidden) // parts + 12 * rows * width,
            transcendentals=rows * hidden // parts,
        ),
        name="gate_back",
    )(low, w_down, gate, up, normed_t, w_gate_up, w_gate_up, total)
    return total, grads[: len(shapes)], grads[len(shapes) :]


def out_kernel(grad_ref, unit_ref, inv_ref, gain_ref, attended_ref, w_ref, one_ref, wide_ref, sums_ref, *rest):
    *grads, acc = rest
    i = pl.program_id(0)
    width = grad_ref.shape[1]

    @pl.when(i == 0)
    def _():
        sums_ref[...] = jnp.zeros_like(sums_ref)
        acc[...] = jnp.zeros_like(acc)

    grad, unit = grad_ref[...], unit_ref[...]
    scaled = grad * gain_ref[...]
    one = inv_ref[:, :1] * (
        scaled - jnp.mean(scaled, -1, keepdims=True) - unit * jnp.mean(scaled * unit, -1, keepdims=True)
    )
    one_ref[...] = one
    sums_ref[0:1, :] += jnp.sum(grad * unit, 0, keepdims=True)
    sums_ref[1:2, :] += jnp.sum(grad, 0, keepdims=True)
    low = one.astype(BF16)
    attended = attended_ref[...]
    acc[...] += dot(attended, low, (0, 0))
    d_attended = dot(low, w_ref[...], (1, 1)).astype(BF16)
    cross = (lax.broadcasted_iota(jnp.int32, (LANES, LANES), 0) < HEAD_DIM) != (lane_of((LANES, LANES)) < HEAD_DIM)
    cross = cross.astype(F32).astype(BF16)
    own_low = lane_of((TILE, LANES)) < HEAD_DIM
    for p in range(width // LANES):
        d = d_attended[:, p * LANES : (p + 1) * LANES]
        product = attended[:, p * LANES : (p + 1) * LANES].astype(F32) * d.astype(F32)
        top = product.astype(BF16)
        delta = dot(top, cross) + dot((product - top.astype(F32)).astype(BF16), cross)
        for h in range(2):
            own = own_low if h == 0 else ~own_low
            at = (2 * p + h) * LANES
            wide_ref[:, at : at + LANES] = with_extras(own, d, delta)

    @pl.when(i == pl.num_programs(0) - 1)
    def _():
        for r in range(0, width, 192):
            emit(acc[r : r + 192, :], r, grads)


def out_back(count, grad, unit, inv, gain, attended, w_out):
    rows, width = grad.shape
    row = lambda columns: pl.BlockSpec((TILE, columns), lambda i: (i, 0))
    fixed = lambda *shape: pl.BlockSpec(shape, lambda i: (0, 0), pipeline_mode=pl.Buffered(1))
    return pl.pallas_call(
        out_kernel,
        grid=(rows // TILE,),
        in_specs=[row(width), row(width), row(LANES), fixed(1, width), row(width), fixed(width, width)],
        out_specs=[row(width), row(2 * width), fixed(8, width)] + split_specs(count, width, width, lambda i: 0),
        out_shape=[
            jax.ShapeDtypeStruct((rows, width), F32),
            jax.ShapeDtypeStruct((rows, 2 * width), BF16),
            jax.ShapeDtypeStruct((8, width), F32),
        ]
        + split_shapes(count, width, width),
        scratch_shapes=[pltpu.VMEM((width, width), F32)],
        compiler_params=params("arbitrary"),
        cost_estimate=pl.CostEstimate(
            flops=4 * rows * width * width, bytes_accessed=20 * rows * width + 6 * width * width, transcendentals=0
        ),
        name="out_back",
    )(grad, unit, inv, gain, attended, w_out)


def attend_back_kernel(
    ends_ref, start_ref, count_ref, query_ref, wide_ref, k_ref, v_ref, cos_ref, sin_ref, cos_all_ref, sin_all_ref,
    out_ref, mask_ref, d_query,
):
    batch, j = pl.program_id(0), pl.program_id(1)
    slots = ends_ref.shape[1]
    width = k_ref.shape[1]
    blocks = query_ref.shape[0] // BLOCK
    start = start_ref[batch, j]
    lane = lane_of((BLOCK, LANES))
    own_low = lane < HEAD_DIM
    units = ((lane & (HEAD_DIM - 1)) < 3).astype(F32).astype(BF16)
    mine = pl.ds(pl.multiple_of(j * BLOCK, BLOCK), BLOCK)

    @pl.when(j == 0)
    def _():
        d_query[...] = jnp.zeros_like(d_query)

    def run(n):
        span = n * BLOCK
        first = pl.multiple_of(start * BLOCK, BLOCK)
        rows = pl.ds(first, span)
        row_segment = segment_of(
            lax.broadcasted_iota(jnp.int32, (BLOCK, LANES), 0) + j * BLOCK, ends_ref, batch, slots
        )
        for t in range(n):
            column = lane + (first + t * BLOCK)
            same = row_segment == segment_of(column, ends_ref, batch, slots)
            mask_ref[:, t * BLOCK : (t + 1) * BLOCK] = jnp.where(same, 0.0, MASKED)

        def pair(p, _):
            at = pl.ds(pl.multiple_of(p * LANES, LANES), LANES)
            k, v = k_ref[:, at], v_ref[:, at]
            d_scores, keys, d_keys, d_values = [], [], [], []
            for h in range(2):
                own = own_low if h == 0 else ~own_low
                head = pl.ds(pl.multiple_of((2 * p + h) * LANES, LANES), LANES)
                query, wide = query_ref[rows, head], wide_ref[rows, head]
                probs = jnp.exp(dot(jnp.where(own, k, units), query, (1, 1)) + mask_ref[:, :span])
                d_probs = dot(jnp.where(own, v, units), wide, (1, 1))
                d_score = (probs * d_probs).astype(BF16)
                d_values.append(dot(probs.astype(BF16), wide))
                d_keys.append(dot(d_score, query))
                d_scores.append(d_score)
                keys.append(jnp.where(own, k, jnp.zeros_like(k)))
            d_query[rows, at] += dot(jnp.concatenate(d_scores, 0), jnp.concatenate(keys, 0), (0, 0))
            d_key = turned(jnp.where(own_low, d_keys[0], d_keys[1]), cos_ref[...], -sin_ref[...])
            out_ref[mine, pl.ds(pl.multiple_of(width + p * LANES, LANES), LANES)] = d_key.astype(BF16)
            d_value = jnp.where(own_low, d_values[0], d_values[1])
            out_ref[mine, pl.ds(pl.multiple_of(2 * width + p * LANES, LANES), LANES)] = d_value.astype(BF16)
            return 0

        lax.fori_loop(0, width // LANES, pair, 0)

    for n in range(1, blocks + 1):
        pl.when(count_ref[batch, j] == n)(functools.partial(run, n))

    @pl.when(j == pl.num_programs(1) - 1)
    def _():
        for p in range(width // LANES):
            part = slice(p * LANES, (p + 1) * LANES)
            out_ref[:, part] = turned(d_query[:, part] * 0.125, cos_all_ref[...], -sin_all_ref[...]).astype(BF16)


def attend_back(ends, starts, counts, query, wide, qkv, cosine, sine):
    rows = qkv.shape[0]
    width = qkv.shape[1] // 3
    batches = ends.shape[0]
    per = rows // batches
    blocks = per // BLOCK
    whole = lambda columns: pl.BlockSpec((per, columns), lambda b, j, *_: (b, 0))
    block = lambda columns, c: pl.BlockSpec((BLOCK, columns), lambda b, j, *_: (b * blocks + j, c))
    return pl.pallas_call(
        attend_back_kernel,
        grid_spec=pltpu.PrefetchScalarGridSpec(
            num_scalar_prefetch=3,
            grid=(batches, blocks),
            in_specs=[
                whole(2 * width), whole(2 * width), block(width, 1), block(width, 2), block(LANES, 0), block(LANES, 0),
                whole(LANES), whole(LANES),
            ],
            out_specs=whole(3 * width),
            scratch_shapes=[pltpu.VMEM((BLOCK, per), F32), pltpu.VMEM((per, width), F32)],
        ),
        out_shape=jax.ShapeDtypeStruct((rows, 3 * width), BF16),
        compiler_params=params("arbitrary", "arbitrary"),
        cost_estimate=pl.CostEstimate(
            flops=30 * rows * per * width, bytes_accessed=18 * rows * width, transcendentals=rows * per * 12
        ),
        name="attend_back",
    )(ends, starts, counts, query, wide, qkv, qkv, cosine, sine, cosine, sine)


def qkv_back_kernel(x_t_ref, d_ref, *grads):
    for r in range(0, x_t_ref.shape[0], 192):
        emit(dot(x_t_ref[r : r + 192, :], d_ref[...]), r, grads)


def qkv_back(count, x_t, d_qkv):
    width, rows = x_t.shape
    columns = d_qkv.shape[1]
    tile = 768
    return pl.pallas_call(
        qkv_back_kernel,
        grid=(columns // tile,),
        in_specs=[
            pl.BlockSpec((width, rows), lambda i: (0, 0), pipeline_mode=pl.Buffered(1)),
            pl.BlockSpec((rows, tile), lambda i: (0, i)),
        ],
        out_specs=split_specs(count, width, tile, lambda i: i),
        out_shape=split_shapes(count, width, columns),
        compiler_params=params("arbitrary"),
        cost_estimate=pl.CostEstimate(
            flops=2 * rows * width * columns, bytes_accessed=2 * rows * columns + 4 * width * columns, transcendentals=0
        ),
        name="qkv_back",
    )(x_t, d_qkv)


def at(array, index):
    return lax.dynamic_index_in_dim(array, index, 1, keepdims=False)


def halves(count, grad):
    if len(grad) == 2:
        return grad
    core = lax.axis_index("dp") & 1
    blocks = grad[0].reshape(count // 2, 2, -1, grad[0].shape[1])
    return at(blocks, core), at(blocks, 1 - core)


def scatter_sum(count, keep, send):
    me = lax.axis_index("dp")
    chips, rows, columns = keep.shape
    core, low, high = me & 1, (me >> 1) & 1, (me >> 2) & 1
    outer = chips // 4

    def swap(array, even_bit, odd_bit):
        pairs = [(i, i ^ (1 << (odd_bit if i & 1 else even_bit))) for i in range(count)]
        return lax.ppermute(array, "dp", pairs)

    keep = keep.reshape(outer, 4, rows, columns)
    got_core = swap(send, 0, 0).reshape(keep.shape)

    def place(first, second):
        return jnp.where(core == 0, second * 2 + first, first * 2 + second)

    mine_first, mine_second = jnp.where(core == 0, low, high), jnp.where(core == 0, high, low)
    sent = jnp.stack(
        [at(keep, place(1 - mine_first, j)) + at(got_core, place(1 - mine_first, j)) for j in range(2)], 1
    )
    got_first = swap(sent, 1, 2)
    other = place(mine_first, 1 - mine_second)
    got_second = swap(at(keep, other) + at(got_core, other) + at(got_first, 1 - mine_second), 2, 1)
    own = place(mine_first, mine_second)
    terms = [at(keep, own), at(got_core, own), at(got_first, mine_second), got_second]
    bit = count.bit_length() - 2
    while outer > 1:
        outer //= 2
        upper = (me >> bit) & 1
        half = lambda array, which: lax.dynamic_slice_in_dim(array, which * outer, outer, 0)
        sent = sum(half(t, 1 - upper) for t in terms)
        terms = [half(t, upper) for t in terms] + [swap(sent, bit, bit)]
        bit -= 1
    return sum(terms).reshape(rows, columns)


def packing(lengths, rows):
    batches, slots = lengths.shape
    index = jnp.arange(rows, dtype=jnp.int32)[None]
    position = jnp.broadcast_to(index, (batches, rows))
    begins = jnp.zeros((batches, rows), jnp.int32)
    ends, start = [], jnp.zeros((batches,), jnp.int32)
    finish = jnp.full((batches, rows), rows, jnp.int32)
    for k in range(slots):
        end = start + lengths[:, k]
        inside = (index >= start[:, None]) & (index < end[:, None])
        position = jnp.where(inside, index - start[:, None], position)
        begins = jnp.where(inside, start[:, None], begins)
        finish = jnp.where(inside, end[:, None], finish)
        ends.append(end)
        start = end
    begins = jnp.where(index >= start[:, None], start[:, None], begins)
    first = begins[:, ::BLOCK] // BLOCK
    last = (finish[:, BLOCK - 1 :: BLOCK] - 1) // BLOCK
    return jnp.stack(ends, 1), position, first, last - first + 1


def rope_tables(position):
    half = HEAD_DIM // 2
    freq = jnp.exp(jnp.arange(half).astype(F32) * (-2.0 * math.log(ROPE_BASE) / HEAD_DIM))
    angle = position.reshape(-1).astype(F32)[:, None] * freq[None, :]
    cosine, sine = jnp.cos(angle), jnp.sin(angle)
    return jnp.concatenate([cosine] * 4, 1), jnp.concatenate([-sine, sine] * 2, 1)


def body(
    tokens, lengths, pairing, w_qkv, w_out, w_gate_up, w_down, norm1_gain, norm1_bias, norm2_gain, norm2_bias
):
    micro, per, width = tokens.shape
    hidden = w_down.shape[0]
    rows = micro * per
    count = lax.axis_size("dp")
    x = tokens.reshape(rows, width)
    gain1, bias1, gain2, bias2 = (p[None, :] for p in (norm1_gain, norm1_bias, norm2_gain, norm2_bias))

    ends, position, starts, counts = packing(lengths, per)
    cosine, sine = rope_tables(position)
    qkv = project(x, w_qkv, cosine, sine)
    attended, query, unit_one, inv_one, normed_low, normed_t = attend(
        ends, starts, counts, qkv, x, w_out, gain1, bias1
    )
    gate, up, act, unit_two, inv_two, activations, pool = feed_forward(
        ends, unit_one, normed_low, w_gate_up, w_down, gain1, bias1, gain2, bias2
    )
    losses, back = contrast(count, pool, lengths, pairing)

    d_two, d_mlp, sums_two, *g_down = down_back(count, ends, unit_two, inv_two, back, gain2, act)
    g_down = scatter_sum(count, *halves(count, g_down))
    parts = 3
    total = d_two
    gates, ups = [], []
    for part in range(parts):
        total, g_gate, g_up = gate_back(
            count, part, parts, d_mlp, w_down, gate, up, normed_t, w_gate_up, total
        )
        gates.append(scatter_sum(count, *halves(count, g_gate)))
        ups.append(scatter_sum(count, *halves(count, g_up)))
    d_one, wide, sums_one, *g_out = out_back(count, total, unit_one, inv_one, gain1, attended, w_out)
    norms = jnp.concatenate([sums_one[:2], sums_two[:2], jnp.zeros((LANES - 4, width), F32)], 0).T
    g_out = halves(count, g_out)
    g_norms = halves(count, [norms])
    g_out = scatter_sum(count, *(jnp.concatenate([a, b], 2) for a, b in zip(g_out, g_norms)))
    d_qkv = attend_back(ends, starts, counts, query, wide, qkv, cosine, sine)
    g_qkv = scatter_sum(count, *halves(count, qkv_back(count, x.T, d_qkv)))
    d_tokens = d_one + jnp.dot(d_qkv, w_qkv.T, preferred_element_type=F32)
    norms = g_out[:, width:].T
    return (
        losses,
        activations.reshape(tokens.shape),
        d_tokens.reshape(tokens.shape),
        g_qkv,
        g_out[:, :width],
        jnp.concatenate(gates + ups, 1),
        g_down,
        norms[0],
        norms[1],
        norms[2],
        norms[3],
    )


def solution(mesh):
    tokens, rows = P(None, "dp", None), P("dp", None)
    return jax.shard_map(
        body,
        mesh=mesh,
        in_specs=(tokens, P(None, "dp"), P(), P(), P(), P(), P(), P(), P(), P(), P()),
        out_specs=(P(), tokens, tokens, rows, rows, rows, rows, P("dp"), P("dp"), P("dp"), P("dp")),
        check_vma=False,
    )
```
